128 devices in a mesh: samp: 2 (over y_lo), vox: 8 (over y_hi, z), chan: 8 (over x, core).
Axes of the slice: x: 4, y: 4 (y_hi: 2, y_lo: 2; y = y_hi * 2 + y_lo), z: 4, core: 2. Of those that a mesh axis runs over, the one named last changes fastest.
Arguments:
- activations: bfloat16 [2, 32, 16, 32, 256], P('samp', 'vox', 'chan'), may hold values from -6 to 6
- out_grad: bfloat16 [2, 32, 16, 32, 512], P('samp', 'vox', None, None, 'chan'), may hold values from -6 to 6
- weight: bfloat16 [27, 256, 512], replicated, may hold values from -0.0546875 to 0.0546875
Outputs:
- data_grad: float32 [2, 32, 16, 32, 256], P('samp', 'vox', None, None, 'chan')
- weight_grad: float32 [27, 256, 512], P(None, 'chan')
The draws below stay inside these ranges and needn't reach their ends.
All inputs are finite; a program needn't handle non-finite values.
Results may differ from the reference program's by a relative error of at most 0.0003.
Values may be sent and summed in bfloat16 or wider, within the bound.
No kernel may reach another device: no remote copies, remote signals or barrier semaphores. Data moves between devices by JAX's collectives and lax.ppermute only.
A program may use at most 192 MiB of HBM per device.

```python
import jax
import jax.numpy as jnp
from jax import lax

CIN = 256
COUT = 512
NY = 16
NZ = 32
SAMPLES = 2
NX = 32


def shard_levels(rng, extent, pieces, smallest, high):
    factor_of, own = 1.0, jax.random.fold_in(rng, 6)
    for position, parts in pieces:
        steps = jnp.exp(jax.random.uniform(jax.random.fold_in(own, position), (parts,), jnp.float32, smallest / len(pieces), high / len(pieces)))
        factor_of = factor_of * jnp.repeat(steps, extent[position] // parts).reshape([-1 if axis == position else 1 for axis in range(len(extent))])
    return factor_of


def normal_values(rng, shape, width, most, split=(), held_as=jnp.bfloat16):
    values = width * jax.random.normal(rng, shape, jnp.float32)
    if split:
        values = values * shard_levels(rng, shape, split, -0.22, 0.18)
    return jnp.clip(values, -most, most).astype(held_as)


def setup_inputs(seed: int = 0) -> dict:
    seeds = jax.random.split(jax.random.key(seed), 4)
    return {
        "activations": normal_values(seeds[0], (SAMPLES, NX, NY, NZ, CIN), 1.0, 6.0, ((0, 2), (1, 8), (2, 8))),
        "out_grad": normal_values(seeds[1], (SAMPLES, NX, NY, NZ, COUT), 1.0, 6.0, ((0, 2), (1, 8), (4, 8))),
        "weight": normal_values(seeds[2], (27, CIN, COUT), (27 * COUT) ** -0.5, 0.0546875),
    }


OFFSETS = [(a, b, c) for a in (-1, 0, 1) for b in (-1, 0, 1) for c in (-1, 0, 1)]


def reference(activations, out_grad, weight):
    samples, size_x, size_y, size_z, channels_in = activations.shape
    channels_out = out_grad.shape[4]
    widths = ((0, 0), (1, 1), (1, 1), (1, 1), (0, 0))
    padded_x = jnp.pad(activations, widths)
    padded_g = jnp.pad(out_grad, widths)
    flat_g = out_grad.reshape(-1, channels_out)
    data_grad = jnp.zeros((flat_g.shape[0], channels_in), jnp.float32)
    blocks = []
    for k, (a, b, c) in enumerate(OFFSETS):
        shifted = padded_x[:, 1 + a:1 + a + size_x, 1 + b:1 + b + size_y, 1 + c:1 + c + size_z].reshape(-1, channels_in)
        blocks.append(lax.dot_general(shifted, flat_g, (((0,), (0,)), ((), ())), preferred_element_type=jnp.float32))
        moved_g = padded_g[:, 1 - a:1 - a + size_x, 1 - b:1 - b + size_y, 1 - c:1 - c + size_z].reshape(-1, channels_out)
        data_grad = data_grad + lax.dot_general(moved_g, weight[k], (((1,), (1,)), ((), ())), preferred_element_type=jnp.float32)
    factor = (samples * size_x * size_y * size_z) ** -0.5
    weight_grad = jnp.stack(blocks) * factor
    return data_grad.reshape(activations.shape), weight_grad
```

```python
import jax
import jax.numpy as jnp
from jax import lax
from jax.experimental import pallas as pl
from jax.experimental.pallas import tpu as pltpu
from jax.sharding import PartitionSpec as P

F32, BF16 = jnp.float32, jnp.bfloat16
STEPS, BIAS = 249.0, 125.0
VM = pl.BlockSpec(memory_space=pltpu.VMEM)
LIMIT = 48 * 1024 * 1024


def call(body, outs, n_in, scratch=(), flops=0, nbytes=1 << 20):
    return pl.pallas_call(
        body,
        out_shape=outs,
        in_specs=[VM] * n_in,
        out_specs=jax.tree.map(lambda _: VM, outs),
        scratch_shapes=list(scratch),
        compiler_params=pltpu.CompilerParams(vmem_limit_bytes=LIMIT),
        cost_estimate=pl.CostEstimate(flops=flops, bytes_accessed=nbytes, transcendentals=0),
    )


def encode(value, exponent):
    q = jnp.sqrt(jnp.abs(value) * jnp.exp2(-exponent)) * STEPS
    whole = jnp.floor(q)
    code = jnp.exp2(whole - BIAS) * (1.0 + (q - whole))
    return jnp.where(value < 0, -code, code).astype(BF16)


def decode(code, exponent):
    code = code.astype(F32)
    size = jnp.abs(code)
    whole = jnp.floor(jnp.log2(size))
    q = (whole + BIAS) + (size * jnp.exp2(-whole) - 1.0)
    square = q * q * (jnp.exp2(exponent) / (STEPS * STEPS))
    return jnp.where(code < 0, -square, square)


def top_exponent(value):
    most = jnp.max(jnp.max(jnp.abs(value), axis=0, keepdims=True), axis=1, keepdims=True)
    return jnp.ceil(jnp.log2(jnp.maximum(most, 1e-30)))


def pack_body(g_ref, x_ref, gs_ref, xs_ref):
    g = g_ref[...]
    for t in range(2):
        gs_ref[512 * t : 512 * (t + 1), :] = jnp.concatenate([g[2 * t], g[2 * t + 1]], axis=1)
    x = x_ref[...]
    for c in range(8):
        xs_ref[c] = jnp.concatenate([x[p, :, 32 * c : 32 * (c + 1)] for p in range(4)], axis=1)


def weight_body(at_ref, w_ref, out_ref):
    none = jnp.zeros((32, 128), BF16)
    for bc in range(9):
        for s in range(4):
            for j in range(4):
                lanes = slice(128 * j, 128 * (j + 1))
                low = w_ref[9 * s + bc, :, lanes] if s < 3 else none
                high = w_ref[9 * (s - 1) + bc, :, lanes] if s > 0 else none
                rows = slice(128 * bc + 32 * s, 128 * bc + 32 * (s + 1))
                out_ref[rows, 256 * j : 256 * j + 128] = jnp.concatenate([low[:, :64], high[:, :64]], axis=1)
                out_ref[rows, 256 * j + 128 : 256 * j + 256] = jnp.concatenate([low[:, 64:], high[:, 64:]], axis=1)


def weights(column, weight):
    return pl.pallas_call(
        weight_body,
        out_shape=jax.ShapeDtypeStruct((1152, 1024), BF16),
        grid_spec=pltpu.PrefetchScalarGridSpec(
            num_scalar_prefetch=1,
            grid=(1,),
            in_specs=[pl.BlockSpec((27, 32, 512), lambda i, at: (0, at[0], 0))],
            out_specs=pl.BlockSpec((1152, 1024), lambda i, at: (0, 0)),
        ),
        compiler_params=pltpu.CompilerParams(vmem_limit_bytes=LIMIT),
        cost_estimate=pl.CostEstimate(flops=0, bytes_accessed=1 << 22, transcendentals=0),
    )(column.reshape(1), weight)


def shifted_z(block, c):
    if c == 0:
        return block
    cells = block.astype(F32).reshape(16, 32, 128)
    edge = jnp.zeros((16, 1, 128), F32)
    moved = [cells[:, 1:], edge] if c > 0 else [edge, cells[:, :31]]
    return jnp.concatenate(moved, axis=1).reshape(512, 128).astype(block.dtype)


def patches_body(x_ref, left_ref, right_ref, out_ref):
    x = x_ref[...]
    pairs = (
        jnp.concatenate([left_ref[:, 96:], x[:, :96]], axis=1),
        jnp.concatenate([x[:, 32:], right_ref[:, :32]], axis=1),
    )
    edge = jnp.zeros((128, 32), BF16)
    for t, block in enumerate(pairs):
        lanes = slice(512 * t, 512 * (t + 1))
        for c in range(3):
            turned = shifted_z(block, c - 1).T
            out_ref[128 * c : 128 * (c + 1), lanes] = jnp.concatenate([edge, turned[:, :480]], axis=1)
            out_ref[128 * (3 + c) : 128 * (4 + c), lanes] = turned
            out_ref[128 * (6 + c) : 128 * (7 + c), lanes] = jnp.concatenate([turned[:, 32:], edge], axis=1)


def gather_panel(spot_ref, parts, panel_ref):
    for i, part in enumerate(parts):
        panel_ref[:, pl.ds(pl.multiple_of(spot_ref[i] * 128, 128), 128)] = part[...]


def kernel_grad_body(spot_ref, l_ref, *refs):
    parts, out_ref, panel_ref, prod_ref = refs[:8], refs[8], refs[9], refs[10]
    gather_panel(spot_ref, parts, panel_ref)
    lane = lax.broadcasted_iota(jnp.int32, (1, 1, 1, 128), 3) < 64
    for j in range(4):
        prod_ref[...] = jnp.dot(l_ref[...], panel_ref[:, 256 * j : 256 * (j + 1)], preferred_element_type=F32)
        even = prod_ref[:, :128].reshape(9, 4, 32, 128)
        odd = prod_ref[:, 128:].reshape(9, 4, 32, 128)
        straight = jnp.where(lane, even[:, 0:3], odd[:, 1:4])
        crossed = jnp.where(lane, odd[:, 0:3], even[:, 1:4])
        total = straight.reshape(864, 128) + pltpu.roll(crossed.reshape(864, 128), 64, 1)
        total = total * (32768.0**-0.5)
        exponent = top_exponent(total)
        code = encode(total, exponent).astype(F32).reshape(27, 4, 8, 128)
        for r in range(4):
            out_ref[4 * r + j, :216, :] = code[:, r].reshape(216, 128).astype(BF16)
            out_ref[4 * r + j, 216:224, :] = jnp.broadcast_to(exponent, (8, 128)).astype(BF16)


def shard_sum_body(in_ref, out_ref):
    total = jnp.zeros((216, 128), F32)
    for i in range(16):
        block = in_ref[i].astype(F32)
        total = total + decode(block[:216], block[216:217, :])
    exponent = top_exponent(total)
    code = jnp.concatenate([encode(total, exponent).astype(F32), jnp.broadcast_to(exponent, (8, 128))], axis=0).astype(BF16)
    for i in range(16):
        out_ref[i] = code


def kernel_out_body(in_ref, out_ref):
    for r in range(4):
        for j in range(4):
            block = in_ref[4 * r + j].astype(F32)
            value = decode(block[:216], block[216:217, :]).reshape(9, 3, 8, 128)
            for a in range(3):
                out_ref[9 * a : 9 * (a + 1), 8 * r : 8 * (r + 1), 128 * j : 128 * (j + 1)] = value[:, a]


def data_grad_body(spot_ref, w_ref, *refs):
    parts, own_ref, low_ref, high_ref, panel_ref, acc_ref = refs[:8], *refs[8:13]
    gather_panel(spot_ref, parts, panel_ref)
    acc_ref[...] = jnp.zeros_like(acc_ref)
    for first in range(0, 9, 2):
        taps = range(first, min(first + 2, 9))
        prod = lax.dot_general(
            panel_ref[...], w_ref[128 * first : 128 * (first + len(taps)), :],
            (((1,), (1,)), ((), ())), preferred_element_type=F32,
        )
        for i, bc in enumerate(taps):
            b, c = bc // 3, bc % 3
            for t in range(2):
                acc_ref[c, t, 32 * b : 32 * b + 512, :] += prod[512 * t : 512 * (t + 1), 128 * i : 128 * (i + 1)]
    sums = []
    for t in range(2):
        sums.append(
            shifted_z(acc_ref[0, t, 32:544, :], 1) + acc_ref[1, t, 32:544, :] + shifted_z(acc_ref[2, t, 32:544, :], -1)
        )
    lane = lax.broadcasted_iota(jnp.int32, (1, 128), 1)
    low, high = sums
    own_ref[...] = jnp.where(lane < 96, pltpu.roll(low, 96, 1), 0.0) + jnp.where(lane >= 32, pltpu.roll(high, 32, 1), 0.0)
    low_ref[...] = jnp.concatenate([low[128 * i : 128 * (i + 1), :32] for i in range(4)], axis=1)
    high_ref[...] = jnp.concatenate([high[128 * i : 128 * (i + 1), 96:] for i in range(4)], axis=1)


def data_out_body(own_ref, low_ref, high_ref, out_ref):
    for p in range(4):
        plane = own_ref[:, 32 * p : 32 * (p + 1)]
        if p in (0, 3):
            extra = low_ref if p == 0 else high_ref
            plane = plane + jnp.concatenate([extra[:, 32 * i : 32 * (i + 1)] for i in range(4)], axis=0)
        out_ref[p] = plane


def on_device(activations, out_grad, weight):
    column = lax.axis_index("chan")
    chip, core = column // 2, column % 2
    struct = jax.ShapeDtypeStruct

    packed_g, packed_x = call(
        pack_body, (struct((1024, 128), BF16), struct((8, 64, 128), BF16)), 2
    )(out_grad.reshape(4, 512, 64), activations.reshape(4, 64, 256))

    def hop(value, chips, cores):
        return lax.ppermute(
            value, "chan", [(i, ((i // 2 + chips) % 4) * 2 + (i % 2 ^ cores)) for i in range(8)]
        )

    mine = [packed_g] + [hop(packed_g, d, 0) for d in (1, 3, 2)]
    parts = mine + [hop(v, 0, 1) for v in mine]
    froms = [chip, (chip + 3) % 4, (chip + 1) % 4, (chip + 2) % 4]
    spots = jnp.stack([2 * f + core for f in froms] + [2 * f + 1 - core for f in froms]).astype(jnp.int32)

    cells = lax.all_to_all(packed_x, "chan", split_axis=0, concat_axis=0, tiled=True).reshape(512, 128)
    left = lax.ppermute(cells, "vox", [(i, i + 1) for i in range(7)])
    right = lax.ppermute(cells, "vox", [(i + 1, i) for i in range(7)])
    patches = call(patches_body, struct((1152, 1024), BF16), 3)(cells, left, right)

    smem = pl.BlockSpec(memory_space=pltpu.SMEM)

    def with_spots(body, outs, scratch, operand, flops):
        return pl.pallas_call(
            body,
            out_shape=outs,
            in_specs=[smem] + [VM] * 9,
            out_specs=jax.tree.map(lambda _: VM, outs),
            scratch_shapes=scratch,
            compiler_params=pltpu.CompilerParams(vmem_limit_bytes=LIMIT),
            cost_estimate=pl.CostEstimate(flops=flops, bytes_accessed=6 << 20, transcendentals=0),
        )(spots, operand, *parts)

    codes = with_spots(
        kernel_grad_body, struct((16, 224, 128), BF16),
        [pltpu.VMEM((1024, 1024), BF16), pltpu.VMEM((1152, 256), F32)], patches, 2 * 1152 * 1024 * 1024,
    )
    own, low, high = with_spots(
        data_grad_body, (struct((512, 128), F32), struct((128, 128), F32), struct((128, 128), F32)),
        [pltpu.VMEM((1024, 1024), BF16), pltpu.VMEM((3, 2, 576, 128), F32)], weights(column, weight), 2 * 1280 * 1024 * 1024,
    )
    swapped = lax.all_to_all(codes, ("samp", "vox"), split_axis=0, concat_axis=0, tiled=True)
    shards = call(shard_sum_body, struct((16, 224, 128), BF16), 1)(swapped)
    final = lax.all_to_all(shards, ("samp", "vox"), split_axis=0, concat_axis=0, tiled=True)
    weight_grad = call(kernel_out_body, struct((27, 32, 512), F32), 1)(final)

    to_high = lax.ppermute(low, "vox", [(i + 1, i) for i in range(7)])
    to_low = lax.ppermute(high, "vox", [(i, i + 1) for i in range(7)])
    data_grad = call(data_out_body, struct((4, 512, 32), F32), 3)(own, to_low, to_high)
    return data_grad.reshape(1, 4, 16, 32, 32), weight_grad


def solution(mesh):
    placed = (P("samp", "vox", "chan", None, None), P("samp", "vox", None, None, "chan"), P())
    return jax.shard_map(
        on_device,
        mesh=mesh,
        in_specs=placed,
        out_specs=(P("samp", "vox", None, None, "chan"), P(None, "chan", None)),
        check_vma=False,
    )
```

```python
import jax
import jax.numpy as jnp
from jax import lax
from jax.experimental import pallas as pl
from jax.experimental.pallas import tpu as pltpu
from jax.sharding import PartitionSpec as P

F32, BF16 = jnp.float32, jnp.bfloat16
STEPS, BIAS = 249.0, 125.0
VM = pl.BlockSpec(memory_space=pltpu.VMEM)
SM = pl.BlockSpec(memory_space=pltpu.SMEM)
ANY = pl.BlockSpec(memory_space=pl.ANY)
HBM = pl.BlockSpec(memory_space=pltpu.HBM)


def call(body, outs, ins, scratch=(), flops=0, nbytes=1 << 20, mib=4):
    return pl.pallas_call(
        body,
        out_shape=outs,
        in_specs=ins,
        out_specs=jax.tree.map(lambda _: VM, outs),
        scratch_shapes=list(scratch),
        compiler_params=pltpu.CompilerParams(vmem_limit_bytes=mib << 20),
        cost_estimate=pl.CostEstimate(flops=flops, bytes_accessed=nbytes, transcendentals=0),
    )


def encode(value, exponent):
    q = jnp.sqrt(jnp.abs(value) * jnp.exp2(-exponent)) * STEPS
    whole = jnp.floor(q)
    code = jnp.exp2(whole - BIAS) * (1.0 + (q - whole))
    return jnp.where(value < 0, -code, code)


def decode(code, exponent):
    size = jnp.abs(code)
    whole = jnp.floor(jnp.log2(size))
    q = (whole + BIAS) + (size * jnp.exp2(-whole) - 1.0)
    square = q * q * (jnp.exp2(exponent) / (STEPS * STEPS))
    return jnp.where(code < 0, -square, square)


def top_exponent(most):
    most = jnp.max(jnp.max(most, axis=0, keepdims=True), axis=1, keepdims=True)
    return jnp.ceil(jnp.log2(jnp.maximum(most, 1e-30)))


def chip_panel(core, own, other):
    return jnp.where(core == 0, jnp.concatenate([own, other], axis=1), jnp.concatenate([other, own], axis=1))


def split_channels(core, block, keep_ref, give_ref):
    for p in range(4):
        rows = block[p]
        even = jnp.concatenate([rows[:, 64 * k : 64 * k + 32] for k in range(4)], axis=1)
        odd = jnp.concatenate([rows[:, 64 * k + 32 : 64 * k + 64] for k in range(4)], axis=1)
        keep_ref[p] = jnp.where(core == 0, even, odd)
        give_ref[p] = jnp.where(core == 0, odd, even)


def first_body(at_ref, g_ref, other_ref, x_ref, panel_ref, low_ref, high_ref, keep_ref, give_ref):
    for p in range(4):
        panel_ref[p] = chip_panel(at_ref[1], g_ref[p], other_ref[p])
    low_ref[...] = panel_ref[0]
    high_ref[...] = panel_ref[3]
    split_channels(at_ref[1], x_ref, keep_ref, give_ref)


def write_patches(panel_ref, left_ref, right_ref, out_ref):
    edge = jnp.zeros((16, 1, 128), F32)
    blank = jnp.zeros((32, 128), BF16)
    for plane in range(-1, 5):
        if plane < 0:
            block = left_ref[...]
        elif plane > 3:
            block = right_ref[...]
        else:
            block = panel_ref[plane]
        cells = block.astype(F32).reshape(16, 32, 128)
        moved = (
            jnp.concatenate([cells[:, 1:], edge], axis=1).reshape(512, 128).astype(BF16),
            block,
            jnp.concatenate([edge, cells[:, :31]], axis=1).reshape(512, 128).astype(BF16),
        )
        for t in range(2):
            slot = plane + 1 - 2 * t
            if not 0 <= slot < 4:
                continue
            rows = 512 * t
            for c in range(3):
                for b in range(3):
                    at = 512 * (3 * b + c) + 128 * slot
                    lanes = slice(at, at + 128)
                    if b == 0:
                        out_ref[rows : rows + 480, lanes] = moved[c][32:]
                        out_ref[rows + 480 : rows + 512, lanes] = blank
                    elif b == 1:
                        out_ref[rows : rows + 512, lanes] = moved[c]
                    else:
                        out_ref[rows : rows + 32, lanes] = blank
                        out_ref[rows + 32 : rows + 512, lanes] = moved[c][:480]


def split_body(at_ref, _, __, *refs):
    blocks, keep_ref, give_ref = refs[:3], refs[3], refs[4]
    for i, block in enumerate(blocks):
        split_channels(at_ref[1], block, keep_ref.at[i], give_ref.at[i])


def kernel_grad_body(spot_ref, p_ref, own_ref, other_ref, keep_ref, got_ref, out_ref, x_ref, xt_ref, sum_ref):
    parts = [own_ref] + [keep_ref.at[i] for i in range(3)] + [other_ref] + [got_ref.at[i] for i in range(3)]
    for i, part in enumerate(parts):
        for p in range(4):
            rows = pl.ds(pl.multiple_of(512 * (p // 2) + spot_ref[i] * 64, 64), 64)
            x_ref[rows, 128 * (p % 2) : 128 * (p % 2) + 128] = part[p]
    for i in range(2):
        xt_ref[128 * i : 128 * (i + 1), :] = x_ref[:, 128 * i : 128 * (i + 1)].T
    most = jnp.zeros((128, 128), F32)
    for bc in range(9):
        prod = jnp.dot(xt_ref[...], p_ref[:, 512 * bc : 512 * (bc + 1)], preferred_element_type=F32)
        for a in range(3):
            even, odd = 128 * (2 - a), 128 * (3 - a)
            total = (prod[:128, even : even + 128] + prod[128:, odd : odd + 128]) * (32768.0**-0.5)
            sum_ref[9 * a + bc] = total
            most = jnp.maximum(most, jnp.abs(total))
    exponent = top_exponent(most)
    for k in range(27):
        sum_ref[k] = encode(sum_ref[k], exponent)
    sum_ref[27] = jnp.full((128, 128), 2.0**-BIAS, F32)
    stamp = jnp.broadcast_to(exponent, (8, 128))
    for jr in range(4):
        for k in range(4):
            rows = slice(32 * k + 8 * jr, 32 * k + 8 * jr + 8)
            for jt in range(4):
                tiles = [sum_ref[7 * jt + i, rows, :] for i in range(7)] + [stamp]
                out_ref[(4 * jr + jt) * 4 + k] = jnp.concatenate(tiles, axis=0).astype(BF16)


def shard_sum_body(in_ref, _, out_ref, sum_ref):
    most = jnp.zeros((56, 128), F32)
    for k in range(4):
        total = jnp.zeros((56, 128), F32)
        for j in range(16):
            code = in_ref[4 * j + k].astype(F32)
            total = total + decode(code[:56], code[56:57])
        sum_ref[k] = total
        most = jnp.maximum(most, jnp.abs(total))
    exponent = top_exponent(most)
    stamp = jnp.broadcast_to(exponent, (8, 128))
    for k in range(4):
        code = jnp.concatenate([encode(sum_ref[k], exponent), stamp], axis=0).astype(BF16)
        for j in range(16):
            out_ref[j, 64 * k : 64 * (k + 1), :] = code


def kernel_out_body(in_ref, out_ref):
    for jr in range(4):
        for jt in range(4):
            for k in range(4):
                code = in_ref[4 * jr + jt, 64 * k : 64 * (k + 1), :].astype(F32)
                value = decode(code[:56], code[56:57])
                for i in range(7 if jt < 3 else 6):
                    out_ref[7 * jt + i, 8 * jr : 8 * jr + 8, 128 * k : 128 * (k + 1)] = value[8 * i : 8 * i + 8]


def data_grad_body(at_ref, panel_ref, left_ref, right_ref, weight_ref, _, *refs):
    outs, cut_ref, w_ref, p_ref, sem = refs[:4], *refs[4:8]
    chip, core = at_ref[0], at_ref[1]
    copy = pltpu.make_async_copy(weight_ref.at[:, :, pl.ds(pl.multiple_of(chip * 128, 128), 128)], cut_ref, sem)
    copy.start()
    write_patches(panel_ref, left_ref, right_ref, p_ref)
    copy.wait()
    none = jnp.zeros((32, 128), BF16)
    for d in range(4):
        rows = pl.ds(pl.multiple_of(64 * lax.rem(chip + d, 4) + 32 * core, 32), 32)
        for bc in range(9):
            for e in range(2):
                for slot in range(4):
                    a = e + 2 - slot
                    lanes = slice(512 * bc + 128 * slot, 512 * bc + 128 * slot + 128)
                    w_ref[128 * e + 32 * d : 128 * e + 32 * d + 32, lanes] = (
                        cut_ref[9 * a + bc, rows, :] if 0 <= a < 3 else none
                    )
    prod = lax.dot_general(p_ref[...], w_ref[...], (((1,), (1,)), ((), ())), preferred_element_type=F32)
    planes = [prod[512 * (p // 2) : 512 * (p // 2) + 512, 128 * (p % 2) : 128 * (p % 2) + 128] for p in range(4)]
    for d, out_ref in enumerate(outs):
        slab = jnp.concatenate([plane[:, 32 * d : 32 * (d + 1)] for plane in planes], axis=1)
        if d == 0:
            out_ref[...] = slab
        else:
            exponent = top_exponent(jnp.abs(slab))
            out_ref[:512, :] = encode(slab, exponent).astype(BF16)
            out_ref[512:, :] = jnp.broadcast_to(exponent, (16, 128)).astype(BF16)


def data_out_body(own_ref, *refs):
    total = own_ref[...]
    for ref in refs[:3]:
        code = ref[...].astype(F32)
        total = total + decode(code[:512], code[512:513])
    for p in range(4):
        refs[3][p] = total[:, 32 * p : 32 * (p + 1)]


def on_device(activations, out_grad, weight):
    column = lax.axis_index("chan")
    chip, core = column // 2, column % 2
    at = jnp.stack([chip, core]).astype(jnp.int32)
    froms = [chip, (chip + 3) % 4, (chip + 1) % 4, (chip + 2) % 4]
    spots = jnp.stack([2 * f + core for f in froms] + [2 * f + 1 - core for f in froms]).astype(jnp.int32)
    struct = jax.ShapeDtypeStruct
    whole = ("samp", "vox", "chan")
    cores = [[8 * j + 2 * k + h for j in range(16) for k in range(4)] for h in range(2)]

    def hop(value, chips, cores):
        return lax.ppermute(
            value, "chan", [(i, ((i // 2 + chips) % 4) * 2 + (i % 2 ^ cores)) for i in range(8)]
        )

    x = activations.reshape(4, 64, 256)
    g = out_grad.reshape(4, 512, 64)
    g_other = hop(g, 0, 1)
    near = [hop(x, d, 0) for d in (1, 3, 2)]
    rim, kept = struct((512, 128), BF16), struct((4, 64, 128), BF16)
    panel, low, high, own, other = call(
        first_body, (struct((4, 512, 128), BF16), rim, rim, kept, kept), [SM, VM, VM, VM]
    )(at, g, g_other, x)
    left = lax.ppermute(high, "vox", [(i, i + 1) for i in range(7)])
    right = lax.ppermute(low, "vox", [(i + 1, i) for i in range(7)])
    other = hop(other, 0, 1)
    three = struct((3, 4, 64, 128), BF16)
    keep, give = call(split_body, (three, three), [SM, ANY, ANY] + [VM] * 3)(at, left, right, *near)
    got = hop(give, 0, 1)
    patches = call(write_patches, struct((1024, 4608), BF16), [VM] * 3)(panel, left, right)

    codes = call(
        kernel_grad_body, struct((64, 64, 128), BF16), [SM] + [VM] * 5,
        [pltpu.VMEM((1024, 256), BF16), pltpu.VMEM((256, 1024), BF16), pltpu.VMEM((28, 128, 128), F32)],
        2 * 2304 * 1024 * 512, 12 << 20, 10,
    )(spots, patches, own, other, keep, got)
    swapped = lax.all_to_all(codes, whole, split_axis=0, concat_axis=0, tiled=True, axis_index_groups=cores)
    slab, coded = struct((512, 128), F32), struct((528, 128), BF16)
    slabs = call(
        data_grad_body, (slab, coded, coded, coded), [SM, VM, VM, VM, HBM, ANY],
        [
            pltpu.VMEM((27, 256, 128), BF16), pltpu.VMEM((256, 4608), BF16), pltpu.VMEM((1024, 4608), BF16),
            pltpu.SemaphoreType.DMA,
        ],
        2 * 2304 * 1024 * 512, 12 << 20, 57,
    )(at, panel, left, right, weight, codes)
    shards = call(
        shard_sum_body, struct((16, 256, 128), BF16), [VM, ANY], [pltpu.VMEM((4, 56, 128), F32)]
    )(swapped, slabs[0])
    final = lax.all_to_all(shards, ("samp", "vox"), split_axis=0, concat_axis=0, tiled=True)
    weight_grad = call(kernel_out_body, struct((27, 32, 512), F32), [VM])(final)
    data_grad = call(data_out_body, struct((4, 512, 32), F32), [VM] * 4)(
        slabs[0], *[hop(slabs[d], d, 0) for d in (1, 3, 2)]
    )
    return data_grad.reshape(1, 4, 16, 32, 32), weight_grad


def solution(mesh):
    placed = (P("samp", "vox", "chan", None, None), P("samp", "vox", None, None, "chan"), P())
    return jax.shard_map(
        on_device,
        mesh=mesh,
        in_specs=placed,
        out_specs=(P("samp", "vox", None, None, "chan"), P(None, "chan", None)),
        check_vma=False,
    )
```

```python
import jax
import jax.numpy as jnp
from jax import lax
from jax.experimental import pallas as pl
from jax.experimental.pallas import tpu as pltpu
from jax.sharding import PartitionSpec as P

F32, BF16 = jnp.float32, jnp.bfloat16
STEPS, BIAS = 249.0, 125.0
TINY = 1024
PAIR = 11070000
VM = pl.BlockSpec(memory_space=pltpu.VMEM)
SM = pl.BlockSpec(memory_space=pltpu.SMEM)
ANY = pl.BlockSpec(memory_space=pl.ANY)
HBM = pl.BlockSpec(memory_space=pltpu.HBM)


def call(body, outs, ins, scratch=(), flops=0, nbytes=1 << 20, mib=4, aliases=None):
    return pl.pallas_call(
        body,
        out_shape=outs,
        in_specs=ins,
        out_specs=jax.tree.map(lambda _: VM, outs),
        scratch_shapes=list(scratch),
        input_output_aliases=aliases or {},
        compiler_params=pltpu.CompilerParams(vmem_limit_bytes=mib << 20),
        cost_estimate=pl.CostEstimate(flops=flops, bytes_accessed=nbytes, transcendentals=0),
    )


def encode(value, exponent):
    size = jnp.abs(value) * jnp.exp2(-exponent) + 1e-30
    code = jnp.exp2(size * lax.rsqrt(size) * STEPS - BIAS)
    return jnp.where(value < 0, -code, code)


def decode(code, exponent):
    q = jnp.log2(jnp.abs(code)) + BIAS
    square = q * q * (jnp.exp2(exponent) / (STEPS * STEPS))
    return jnp.where(code < 0, -square, square)


def top_exponent(most):
    most = jnp.max(jnp.max(most, axis=0, keepdims=True), axis=1, keepdims=True)
    return jnp.ceil(jnp.log2(jnp.maximum(most, 1e-30)))


def chip_panel(core, own, other):
    return jnp.where(core == 0, jnp.concatenate([own, other], axis=1), jnp.concatenate([other, own], axis=1))


def split_channels(core, block, keep_ref, give_ref):
    for p in range(4):
        rows = block[p]
        even = jnp.concatenate([rows[:, 64 * k : 64 * k + 32] for k in range(4)], axis=1)
        odd = jnp.concatenate([rows[:, 64 * k + 32 : 64 * k + 64] for k in range(4)], axis=1)
        keep_ref[p] = jnp.where(core == 0, even, odd)
        give_ref[p] = jnp.where(core == 0, odd, even)


def pack_body(g_ref, panel_ref, low_ref, high_ref):
    for p in range(4):
        panel_ref[p] = jnp.concatenate([g_ref[p, :256], g_ref[p, 256:]], axis=1)
    low_ref[...] = panel_ref[0]
    high_ref[...] = panel_ref[3]


def write_plane(at_ref, own, other, out_ref, lane):
    halves = [chip_panel(at_ref[1], own[:, i : i + 64], other[:, i : i + 64]) for i in (0, 64)]
    block = jnp.concatenate(halves, axis=0)
    edge = jnp.zeros((16, 1, 128), F32)
    blank = jnp.zeros((32, 128), BF16)
    cells = block.astype(F32).reshape(16, 32, 128)
    moved = (
        jnp.concatenate([cells[:, 1:], edge], axis=1).reshape(512, 128).astype(BF16),
        block,
        jnp.concatenate([edge, cells[:, :31]], axis=1).reshape(512, 128).astype(BF16),
    )
    for c in range(3):
        out_ref[c, 0:32, lane : lane + 128] = blank
        out_ref[c, 32:544, lane : lane + 128] = moved[c]
        out_ref[c, 544:576, lane : lane + 128] = blank


def inner_body(at_ref, panel_ref, other_ref, x_ref, out_ref, keep_ref, give_ref, token_ref):
    for p in range(4):
        keep_ref[p] = split_channels(at_ref[1], x_ref[p], True)
        give_ref[p] = split_channels(at_ref[1], x_ref[p], False)
    for p in range(4):
        write_plane(at_ref, panel_ref[p], other_ref[p], out_ref, 128 * p)
    token_ref[...] = jnp.zeros((8, 128), F32)


def write_edges(at_ref, inner_ref, rims, edge_ref):
    edge_ref[0, :, :, 128:] = inner_ref[:, :, :128]
    edge_ref[1, :, :, :128] = inner_ref[:, :, 384:]
    write_plane(at_ref, rims[0][0], rims[1][0], edge_ref.at[0], 0)
    write_plane(at_ref, rims[0][1], rims[1][1], edge_ref.at[1], 128)


def patches(inner_ref, edge_ref, t, i, bc):
    window = slice(64 - 32 * (bc // 3), 576 - 32 * (bc // 3))
    return inner_ref[bc % 3, window, 128:384] if t != i else edge_ref[t, bc % 3, window, :]


def split_channels(core, block, own):
    parts = [
        jnp.concatenate([block[:, 64 * k + 32 * h : 64 * k + 32 * h + 32] for k in range(4)], axis=1) for h in range(2)
    ]
    return jnp.where((core == 0) == own, parts[0], parts[1])


def pair_body(left_ref, right_ref, out_ref):
    out_ref[0] = left_ref[...]
    out_ref[1] = right_ref[...]


def give_body(at_ref, _, *refs):
    for i in range(3):
        for p in range(4):
            refs[3][i, p] = split_channels(at_ref[1], refs[i][p], False)


def kernel_grad_body(spot_ref, at_ref, inner_ref, *refs):
    rims, keep_ref, blocks, own_got_ref, got_ref, out_ref, token_ref, edge_ref, x_ref, xt_ref, sum_ref = (
        refs[:2], refs[2], refs[3:6], *refs[6:]
    )
    write_edges(at_ref, inner_ref, rims, edge_ref)
    for i in range(8):
        for p in range(4):
            if i % 4 == 0:
                part = (own_got_ref if i else keep_ref)[p]
            else:
                part = split_channels(at_ref[1], blocks[i - 1][p], True) if i < 4 else got_ref[i - 5, p]
            rows = pl.ds(pl.multiple_of(512 * (p // 2) + spot_ref[i] * 64, 64), 64)
            x_ref[rows, 128 * (p % 2) : 128 * (p % 2) + 128] = part
    token_ref[...] = jnp.zeros((8, 128), F32)
    for i in range(2):
        xt_ref[128 * i : 128 * (i + 1), :] = x_ref[:, 128 * i : 128 * (i + 1)].T
    most = jnp.zeros((128, 128), F32)
    for bc in range(9):
        prod = jnp.concatenate([
            sum(
                jnp.dot(
                    xt_ref[:, 512 * t : 512 * (t + 1)], patches(inner_ref, edge_ref, t, i, bc), preferred_element_type=F32
                )
                for t in range(2)
            )
            for i in range(2)
        ], axis=1)
        for a in range(3):
            even, odd = 128 * (2 - a), 128 * (3 - a)
            total = (prod[:128, even : even + 128] + prod[128:, odd : odd + 128]) * (32768.0**-0.5)
            sum_ref[9 * a + bc] = total
            most = jnp.maximum(most, jnp.abs(total))
    exponent = top_exponent(most)
    for k in range(27):
        sum_ref[k] = encode(sum_ref[k], exponent)
    stamp = jnp.broadcast_to(exponent, (2, 128))
    for jr in range(4):
        for k in range(4):
            rows = slice(32 * k + 8 * jr, 32 * k + 8 * jr + 8)
            rest = jnp.concatenate([sum_ref[24 + i, rows, :] for i in range(3)], axis=0)
            for jt in range(4):
                tiles = [sum_ref[6 * jt + i, rows, :] for i in range(6)] + [rest[6 * jt : 6 * jt + 6], stamp]
                out_ref[(4 * jr + jt) * 4 + k] = jnp.concatenate(tiles, axis=0).astype(BF16)


def shard_sum_body(in_ref, _, out_ref, sum_ref):
    used = lax.broadcasted_iota(jnp.int32, (56, 128), 0) < 54
    most = jnp.zeros((56, 128), F32)
    for k in range(4):
        total = jnp.zeros((56, 128), F32)
        for j in range(16):
            code = in_ref[4 * j + k].astype(F32)
            total = total + decode(code, code[54:55])
        total = jnp.where(used, total, 0.0)
        sum_ref[k] = total
        most = jnp.maximum(most, jnp.abs(total))
    exponent = top_exponent(most)
    for k in range(4):
        code = jnp.where(used, encode(sum_ref[k], exponent), exponent).astype(BF16)
        for j in range(16):
            out_ref[j, k] = code


def kernel_out_body(in_ref, out_ref):
    for jr in range(4):
        for k in range(4):
            at = (slice(8 * jr, 8 * jr + 8), slice(128 * k, 128 * (k + 1)))
            rest = []
            for jt in range(4):
                code = in_ref[4 * jr + jt, k].astype(F32)
                value = decode(code, code[54:55])
                for i in range(6):
                    out_ref[6 * jt + i, at[0], at[1]] = value[8 * i : 8 * i + 8]
                rest.append(value[48:54])
            rest = jnp.concatenate(rest, axis=0)
            for i in range(3):
                out_ref[24 + i, at[0], at[1]] = rest[8 * i : 8 * i + 8]


def data_grad_body(at_ref, inner_ref, rims_ref, rims_other_ref, weight_ref, _, *refs):
    outs, token_ref, cut_ref, w_ref, edge_ref, sem = refs[:4], *refs[4:9]
    chip, core = at_ref[0], at_ref[1]
    copy = pltpu.make_async_copy(weight_ref.at[:, :, pl.ds(pl.multiple_of(chip * 128, 128), 128)], cut_ref, sem)
    copy.start()
    write_edges(at_ref, inner_ref, (rims_ref, rims_other_ref), edge_ref)
    token_ref[...] = jnp.zeros((8, 128), F32)
    copy.wait()
    none = jnp.zeros((32, 128), BF16)
    for d in range(4):
        rows = pl.ds(pl.multiple_of(64 * lax.rem(chip + d, 4) + 32 * core, 32), 32)
        for bc in range(9):
            for e in range(2):
                for slot in range(4):
                    a = e + 2 - slot
                    lanes = slice(512 * bc + 128 * slot, 512 * bc + 128 * slot + 128)
                    w_ref[128 * e + 32 * d : 128 * e + 32 * d + 32, lanes] = (
                        cut_ref[9 * a + bc, rows, :] if 0 <= a < 3 else none
                    )
    planes = []
    for t in range(2):
        prod = jnp.zeros((512, 256), F32)
        for bc in range(9):
            for i in range(2):
                prod = prod + lax.dot_general(
                    patches(inner_ref, edge_ref, t, i, bc), w_ref[:, 512 * bc + 256 * i : 512 * bc + 256 * i + 256],
                    (((1,), (1,)), ((), ())), preferred_element_type=F32,
                )
        planes += [prod[:, :128], prod[:, 128:]]
    for d, out_ref in enumerate(outs):
        slab = jnp.concatenate([plane[:, 32 * d : 32 * (d + 1)] for plane in planes], axis=1)
        if d == 0:
            out_ref[...] = slab
        else:
            exponent = top_exponent(jnp.abs(slab))
            out_ref[:512, :] = encode(slab, exponent).astype(BF16)
            out_ref[512:, :] = jnp.broadcast_to(exponent, (16, 128)).astype(BF16)


def data_out_body(own_ref, *refs):
    total = own_ref[...]
    for ref in refs[:3]:
        code = ref[...].astype(F32)
        total = total + decode(code[:512], code[512:513])
    for p in range(4):
        refs[3][p] = total[:, 32 * p : 32 * (p + 1)]


def on_device(activations, out_grad, weight):
    column = lax.axis_index("chan")
    chip, core = column // 2, column % 2
    at = jnp.stack([chip, core]).astype(jnp.int32)
    froms = [chip, (chip + 3) % 4, (chip + 1) % 4, (chip + 2) % 4]
    spots = jnp.stack([2 * f + core for f in froms] + [2 * f + 1 - core for f in froms]).astype(jnp.int32)
    struct = jax.ShapeDtypeStruct
    whole = ("samp", "vox", "chan")
    cores = [[8 * j + 2 * k + h for j in range(16) for k in range(4)] for h in range(2)]

    def hop(value, chips, cores):
        return lax.ppermute(
            value, "chan", [(i, ((i // 2 + chips) % 4) * 2 + (i % 2 ^ cores)) for i in range(8)]
        )

    x = activations.reshape(4, 64, 256)
    g = out_grad.reshape(4, 512, 64)
    near = [hop(x, d, 0) for d in (1, 3, 2)]
    rim, token = struct((256, 128), BF16), struct((8, 128), F32)
    panel, low, high = call(pack_body, (struct((4, 256, 128), BF16), rim, rim), [VM])(g)
    left = lax.ppermute(high, "vox", [(i, i + 1) for i in range(7)])
    right = lax.ppermute(low, "vox", [(i + 1, i) for i in range(7)])
    other = hop(panel, 0, 1)
    rims = call(pair_body, struct((2, 256, 128), BF16), [VM, VM], nbytes=PAIR)(left, right)
    rims = [rims, hop(rims, 0, 1)]
    kept = struct((4, 64, 128), BF16)
    inner, keep, own_give, built = call(
        inner_body, (struct((3, 576, 512), BF16), kept, kept, token), [SM, VM, VM, VM], nbytes=TINY
    )(at, panel, other, x)
    own_got = hop(own_give, 0, 1)
    give = call(give_body, struct((3, 4, 64, 128), BF16), [SM, VM] + [VM] * 3, nbytes=TINY)(at, built, *near)
    got = hop(give, 0, 1)

    edges = pltpu.VMEM((2, 3, 576, 256), BF16)
    codes, made = call(
        kernel_grad_body, (struct((64, 56, 128), BF16), token), [SM, SM] + [VM] * 9,
        [edges, pltpu.VMEM((1024, 256), BF16), pltpu.VMEM((256, 1024), BF16), pltpu.VMEM((27, 128, 128), F32)],
        2 * 2304 * 1024 * 512, 12 << 20, 12,
    )(spots, at, inner, *rims, keep, *near, own_got, got)
    swapped = lax.all_to_all(codes, whole, split_axis=0, concat_axis=0, tiled=True, axis_index_groups=cores)
    slab, coded = struct((512, 128), F32), struct((528, 128), BF16)
    *slabs, done = call(
        data_grad_body, (slab, coded, coded, coded, token), [SM] + [VM] * 3 + [HBM, VM],
        [pltpu.VMEM((27, 256, 128), BF16), pltpu.VMEM((256, 4608), BF16), edges, pltpu.SemaphoreType.DMA],
        2 * 2304 * 1024 * 512, 12 << 20, 24,
    )(at, inner, *rims, weight, made)
    shards = call(
        shard_sum_body, struct((16, 4, 56, 128), BF16), [VM, VM], [pltpu.VMEM((4, 56, 128), F32)]
    )(swapped, done)
    final = lax.all_to_all(shards, ("samp", "vox"), split_axis=0, concat_axis=0, tiled=True)
    weight_grad = call(kernel_out_body, struct((27, 32, 512), F32), [VM])(final)
    data_grad = call(data_out_body, struct((4, 512, 32), F32), [VM] * 4)(
        slabs[0], *[hop(slabs[d], d, 0) for d in (1, 3, 2)]
    )
    return data_grad.reshape(1, 4, 16, 32, 32), weight_grad


def solution(mesh):
    placed = (P("samp", "vox", "chan", None, None), P("samp", "vox", None, None, "chan"), P())
    return jax.shard_map(
        on_device,
        mesh=mesh,
        in_specs=placed,
        out_specs=(P("samp", "vox", None, None, "chan"), P(None, "chan", None)),
        check_vma=False,
    )
```

```python
import jax
import jax.numpy as jnp
from jax import lax
from jax.experimental import pallas as pl
from jax.experimental.pallas import tpu as pltpu
from jax.sharding import PartitionSpec as P

F32, BF16 = jnp.float32, jnp.bfloat16
STEPS, BIAS = 249.0, 125.0
TINY = 1024
PAIR = 11070000
VM = pl.BlockSpec(memory_space=pltpu.VMEM)
HBM = pl.BlockSpec(memory_space=pltpu.HBM)


def place():
    chan = lax.axis_index("chan")
    return lax.div(chan, 2), lax.rem(chan, 2), lax.rem(lax.axis_index("vox"), 2)


def call(body, outs, ins, scratch=(), flops=0, nbytes=1 << 20, mib=4, aliases=None):
    return pl.pallas_call(
        body,
        out_shape=outs,
        in_specs=ins,
        out_specs=jax.tree.map(lambda _: VM, outs),
        scratch_shapes=list(scratch),
        input_output_aliases=aliases or {},
        compiler_params=pltpu.CompilerParams(vmem_limit_bytes=mib << 20),
        cost_estimate=pl.CostEstimate(flops=flops, bytes_accessed=nbytes, transcendentals=0),
    )


def encode(value, exponent):
    size = jnp.abs(value) * jnp.exp2(-exponent) + 1e-30
    code = jnp.exp2(size * lax.rsqrt(size) * STEPS - BIAS)
    return jnp.where(value < 0, -code, code)


def decode(code, exponent):
    q = jnp.log2(jnp.abs(code)) + BIAS
    square = q * q * (jnp.exp2(exponent) / (STEPS * STEPS))
    return jnp.where(code < 0, -square, square)


def top_exponent(most):
    most = jnp.max(jnp.max(most, axis=0, keepdims=True), axis=1, keepdims=True)
    return jnp.ceil(jnp.log2(jnp.maximum(most, 1e-30)))


def chip_panel(core, own, other):
    return jnp.where(core == 0, jnp.concatenate([own, other], axis=1), jnp.concatenate([other, own], axis=1))


def split_channels(core, block, keep_ref, give_ref):
    for p in range(4):
        rows = block[p]
        even = jnp.concatenate([rows[:, 64 * k : 64 * k + 32] for k in range(4)], axis=1)
        odd = jnp.concatenate([rows[:, 64 * k + 32 : 64 * k + 64] for k in range(4)], axis=1)
        keep_ref[p] = jnp.where(core == 0, even, odd)
        give_ref[p] = jnp.where(core == 0, odd, even)


def pack_body(g_ref, panel_ref, low_ref, high_ref):
    odd = place()[2] == 1
    for p in range(4):
        panel_ref[p] = jnp.concatenate([g_ref[p, :256], g_ref[p, 256:]], axis=1)
    low_ref[...] = jnp.where(odd, panel_ref[3], panel_ref[0])
    high_ref[...] = jnp.where(odd, panel_ref[0], panel_ref[3])


def write_plane(own, other, out_ref, lane):
    halves = [chip_panel(place()[1], own[:, i : i + 64], other[:, i : i + 64]) for i in (0, 64)]
    block = jnp.concatenate(halves, axis=0)
    edge = jnp.zeros((16, 1, 128), F32)
    blank = jnp.zeros((32, 128), BF16)
    cells = block.astype(F32).reshape(16, 32, 128)
    moved = (
        jnp.concatenate([cells[:, 1:], edge], axis=1).reshape(512, 128).astype(BF16),
        block,
        jnp.concatenate([edge, cells[:, :31]], axis=1).reshape(512, 128).astype(BF16),
    )
    for c in range(3):
        out_ref[c, 0:32, lane : lane + 128] = blank
        out_ref[c, 32:544, lane : lane + 128] = moved[c]
        out_ref[c, 544:576, lane : lane + 128] = blank


def inner_body(panel_ref, other_ref, x_ref, out_ref, keep_ref, give_ref, token_ref):
    for p in range(4):
        keep_ref[p] = split_channels(place()[1], x_ref[p], True)
        give_ref[p] = split_channels(place()[1], x_ref[p], False)
    for p in range(4):
        write_plane(panel_ref[p], other_ref[p], out_ref, 128 * p)
    token_ref[...] = jnp.zeros((8, 128), F32)


def write_edges(inner_ref, rims, edge_ref):
    edge_ref[0, :, :, 128:] = inner_ref[:, :, :128]
    edge_ref[1, :, :, :128] = inner_ref[:, :, 384:]
    write_plane(rims[0][0], rims[1][0], edge_ref.at[0], 0)
    write_plane(rims[0][1], rims[1][1], edge_ref.at[1], 128)


def patches(inner_ref, edge_ref, t, i, bc):
    window = slice(64 - 32 * (bc // 3), 576 - 32 * (bc // 3))
    return inner_ref[bc % 3, window, 128:384] if t != i else edge_ref[t, bc % 3, window, :]


def split_channels(core, block, own):
    parts = [
        jnp.concatenate([block[:, 64 * k + 32 * h : 64 * k + 32 * h + 32] for k in range(4)], axis=1) for h in range(2)
    ]
    return jnp.where((core == 0) == own, parts[0], parts[1])


def pair_body(first_ref, second_ref, out_ref):
    odd = place()[2] == 1
    out_ref[0] = jnp.where(odd, second_ref[...], first_ref[...])
    out_ref[1] = jnp.where(odd, first_ref[...], second_ref[...])


def give_body(_, *refs):
    for i in range(3):
        for p in range(4):
            refs[3][i, p] = split_channels(place()[1], refs[i][p], False)


def kernel_grad_body(inner_ref, *refs):
    rims, keep_ref, blocks, own_got_ref, got_ref, out_ref, token_ref, edge_ref, x_ref, xt_ref, sum_ref = (
        refs[:2], refs[2], refs[3:6], *refs[6:]
    )
    write_edges(inner_ref, rims, edge_ref)
    chip, core, _ = place()
    for i in range(8):
        spot = 2 * lax.rem(chip + (0, 3, 1, 2)[i % 4], 4) + (core if i < 4 else 1 - core)
        for p in range(4):
            if i % 4 == 0:
                part = (own_got_ref if i else keep_ref)[p]
            else:
                part = split_channels(place()[1], blocks[i - 1][p], True) if i < 4 else got_ref[i - 5, p]
            rows = pl.ds(pl.multiple_of(512 * (p // 2) + spot * 64, 64), 64)
            x_ref[rows, 128 * (p % 2) : 128 * (p % 2) + 128] = part
    token_ref[...] = jnp.zeros((8, 128), F32)
    for i in range(2):
        xt_ref[128 * i : 128 * (i + 1), :] = x_ref[:, 128 * i : 128 * (i + 1)].T
    most = jnp.zeros((128, 128), F32)
    for bc in range(9):
        prod = jnp.concatenate([
            sum(
                jnp.dot(
                    xt_ref[:, 512 * t : 512 * (t + 1)], patches(inner_ref, edge_ref, t, i, bc), preferred_element_type=F32
                )
                for t in range(2)
            )
            for i in range(2)
        ], axis=1)
        for a in range(3):
            even, odd = 128 * (2 - a), 128 * (3 - a)
            total = (prod[:128, even : even + 128] + prod[128:, odd : odd + 128]) * (32768.0**-0.5)
            sum_ref[9 * a + bc] = total
            most = jnp.maximum(most, jnp.abs(total))
    exponent = top_exponent(most)
    for k in range(27):
        sum_ref[k] = encode(sum_ref[k], exponent)
    stamp = jnp.broadcast_to(exponent, (2, 128))
    for jr in range(4):
        for k in range(4):
            rows = slice(32 * k + 8 * jr, 32 * k + 8 * jr + 8)
            rest = jnp.concatenate([sum_ref[24 + i, rows, :] for i in range(3)], axis=0)
            for jt in range(4):
                tiles = [sum_ref[6 * jt + i, rows, :] for i in range(6)] + [rest[6 * jt : 6 * jt + 6], stamp]
                out_ref[(4 * jr + jt) * 4 + k] = jnp.concatenate(tiles, axis=0).astype(BF16)


def shard_sum_body(in_ref, _, out_ref, sum_ref):
    used = lax.broadcasted_iota(jnp.int32, (56, 128), 0) < 54
    most = jnp.zeros((56, 128), F32)
    for k in range(4):
        total = jnp.zeros((56, 128), F32)
        for j in range(16):
            code = in_ref[4 * j + k].astype(F32)
            total = total + decode(code, code[54:55])
        total = jnp.where(used, total, 0.0)
        sum_ref[k] = total
        most = jnp.maximum(most, jnp.abs(total))
    exponent = top_exponent(most)
    for k in range(4):
        code = jnp.where(used, encode(sum_ref[k], exponent), exponent).astype(BF16)
        for j in range(16):
            out_ref[j, k] = code


def kernel_out_body(in_ref, out_ref):
    for jr in range(4):
        for k in range(4):
            at = (slice(8 * jr, 8 * jr + 8), slice(128 * k, 128 * (k + 1)))
            rest = []
            for jt in range(4):
                code = in_ref[4 * jr + jt, k].astype(F32)
                value = decode(code, code[54:55])
                for i in range(6):
                    out_ref[6 * jt + i, at[0], at[1]] = value[8 * i : 8 * i + 8]
                rest.append(value[48:54])
            rest = jnp.concatenate(rest, axis=0)
            for i in range(3):
                out_ref[24 + i, at[0], at[1]] = rest[8 * i : 8 * i + 8]


def data_grad_body(inner_ref, rims_ref, rims_other_ref, weight_ref, _, *refs):
    outs, token_ref, cut_ref, w_ref, edge_ref, sem = refs[:4], *refs[4:9]
    chip, core, _ = place()
    copy = pltpu.make_async_copy(weight_ref.at[:, :, pl.ds(pl.multiple_of(chip * 128, 128), 128)], cut_ref, sem)
    copy.start()
    write_edges(inner_ref, (rims_ref, rims_other_ref), edge_ref)
    token_ref[...] = jnp.zeros((8, 128), F32)
    copy.wait()
    none = jnp.zeros((32, 128), BF16)
    for d in range(4):
        rows = pl.ds(pl.multiple_of(64 * lax.rem(chip + d, 4) + 32 * core, 32), 32)
        for bc in range(9):
            for e in range(2):
                for slot in range(4):
                    a = e + 2 - slot
                    lanes = slice(512 * bc + 128 * slot, 512 * bc + 128 * slot + 128)
                    w_ref[128 * e + 32 * d : 128 * e + 32 * d + 32, lanes] = (
                        cut_ref[9 * a + bc, rows, :] if 0 <= a < 3 else none
                    )
    planes = []
    for t in range(2):
        prod = jnp.zeros((512, 256), F32)
        for bc in range(9):
            for i in range(2):
                prod = prod + lax.dot_general(
                    patches(inner_ref, edge_ref, t, i, bc), w_ref[:, 512 * bc + 256 * i : 512 * bc + 256 * i + 256],
                    (((1,), (1,)), ((), ())), preferred_element_type=F32,
                )
        planes += [prod[:, :128], prod[:, 128:]]
    for d, out_ref in enumerate(outs):
        slab = jnp.concatenate([plane[:, 32 * d : 32 * (d + 1)] for plane in planes], axis=1)
        if d == 0:
            out_ref[...] = slab
        else:
            exponent = top_exponent(jnp.abs(slab))
            out_ref[:512, :] = encode(slab, exponent).astype(BF16)
            out_ref[512:, :] = jnp.broadcast_to(exponent, (16, 128)).astype(BF16)


def data_out_body(own_ref, *refs):
    total = own_ref[...]
    for ref in refs[:3]:
        code = ref[...].astype(F32)
        total = total + decode(code[:512], code[512:513])
    for p in range(4):
        refs[3][p] = total[:, 32 * p : 32 * (p + 1)]


def on_device(activations, out_grad, weight):
    struct = jax.ShapeDtypeStruct
    whole = ("samp", "vox", "chan")
    cores = [[8 * j + 2 * k + h for j in range(16) for k in range(4)] for h in range(2)]

    def hop(value, chips, cores):
        return lax.ppermute(
            value, "chan", [(i, ((i // 2 + chips) % 4) * 2 + (i % 2 ^ cores)) for i in range(8)]
        )

    x = activations.reshape(4, 64, 256)
    g = out_grad.reshape(4, 512, 64)
    near = [hop(x, d, 0) for d in (1, 3, 2)]
    rim, token = struct((256, 128), BF16), struct((8, 128), F32)
    panel, low, high = call(pack_body, (struct((4, 256, 128), BF16), rim, rim), [VM])(g)
    left = lax.ppermute(low, "vox", [swap for i in (1, 3, 5) for swap in ((i, i + 1), (i + 1, i))])
    right = lax.ppermute(high, "vox", [swap for i in (0, 2, 4, 6) for swap in ((i, i + 1), (i + 1, i))])
    other = hop(panel, 0, 1)
    rims = call(pair_body, struct((2, 256, 128), BF16), [VM, VM], nbytes=PAIR)(left, right)
    rims = [rims, hop(rims, 0, 1)]
    kept = struct((4, 64, 128), BF16)
    inner, keep, own_give, built = call(
        inner_body, (struct((3, 576, 512), BF16), kept, kept, token), [VM, VM, VM], nbytes=TINY
    )(panel, other, x)
    own_got = hop(own_give, 0, 1)
    give = call(give_body, struct((3, 4, 64, 128), BF16), [VM] * 4, nbytes=TINY)(built, *near)
    got = hop(give, 0, 1)

    edges = pltpu.VMEM((2, 3, 576, 256), BF16)
    codes, made = call(
        kernel_grad_body, (struct((64, 56, 128), BF16), token), [VM] * 9,
        [edges, pltpu.VMEM((1024, 256), BF16), pltpu.VMEM((256, 1024), BF16), pltpu.VMEM((27, 128, 128), F32)],
        2 * 2304 * 1024 * 512, 12 << 20, 12,
    )(inner, *rims, keep, *near, own_got, got)
    swapped = lax.all_to_all(codes, whole, split_axis=0, concat_axis=0, tiled=True, axis_index_groups=cores)
    slab, coded = struct((512, 128), F32), struct((528, 128), BF16)
    *slabs, done = call(
        data_grad_body, (slab, coded, coded, coded, token), [VM] * 3 + [HBM, VM],
        [pltpu.VMEM((27, 256, 128), BF16), pltpu.VMEM((256, 4608), BF16), edges, pltpu.SemaphoreType.DMA],
        2 * 2304 * 1024 * 512, 12 << 20, 24,
    )(inner, *rims, weight, made)
    shards = call(
        shard_sum_body, struct((16, 4, 56, 128), BF16), [VM, VM], [pltpu.VMEM((4, 56, 128), F32)]
    )(swapped, done)
    final = lax.all_to_all(shards, ("samp", "vox"), split_axis=0, concat_axis=0, tiled=True)
    weight_grad = call(kernel_out_body, struct((27, 32, 512), F32), [VM])(final)
    data_grad = call(data_out_body, struct((4, 512, 32), F32), [VM] * 4)(
        slabs[0], *[hop(slabs[d], d, 0) for d in (1, 3, 2)]
    )
    return data_grad.reshape(1, 4, 16, 32, 32), weight_grad


def solution(mesh):
    placed = (P("samp", "vox", "chan", None, None), P("samp", "vox", None, None, "chan"), P())
    return jax.shard_map(
        on_device,
        mesh=mesh,
        in_specs=placed,
        out_specs=(P("samp", "vox", None, None, "chan"), P(None, "chan", None)),
        check_vma=False,
    )
```

```python
import jax
import jax.numpy as jnp
from jax import lax
from jax.experimental import pallas as pl
from jax.experimental.pallas import tpu as pltpu
from jax.sharding import PartitionSpec as P

F32, BF16 = jnp.float32, jnp.bfloat16
STEPS, BIAS = 249.0, 125.0
TINY = 1024
PAIR = 11070000
VM = pl.BlockSpec(memory_space=pltpu.VMEM)
HBM = pl.BlockSpec(memory_space=pltpu.HBM)


def place():
    chan = lax.axis_index("chan")
    return lax.div(chan, 2), lax.rem(chan, 2), lax.rem(lax.axis_index("vox"), 2)


def call(body, outs, ins, scratch=(), flops=0, nbytes=1 << 20, mib=4, aliases=None):
    return pl.pallas_call(
        body,
        out_shape=outs,
        in_specs=ins,
        out_specs=jax.tree.map(lambda _: VM, outs),
        scratch_shapes=list(scratch),
        input_output_aliases=aliases or {},
        compiler_params=pltpu.CompilerParams(vmem_limit_bytes=mib << 20),
        cost_estimate=pl.CostEstimate(flops=flops, bytes_accessed=nbytes, transcendentals=0),
    )


def encode(value, exponent):
    size = jnp.abs(value) * jnp.exp2(-exponent) + 1e-30
    code = jnp.exp2(size * lax.rsqrt(size) * STEPS - BIAS)
    return jnp.where(value < 0, -code, code)


def decode(code, exponent):
    q = jnp.log2(jnp.abs(code)) + BIAS
    square = q * q * (jnp.exp2(exponent) / (STEPS * STEPS))
    return jnp.where(code < 0, -square, square)


def top_exponent(most):
    most = jnp.max(jnp.max(most, axis=0, keepdims=True), axis=1, keepdims=True)
    return jnp.ceil(jnp.log2(jnp.maximum(most, 1e-30)))


def chip_panel(core, own, other):
    return jnp.where(core == 0, jnp.concatenate([own, other], axis=1), jnp.concatenate([other, own], axis=1))


def split_channels(core, block, keep_ref, give_ref):
    for p in range(4):
        rows = block[p]
        even = jnp.concatenate([rows[:, 64 * k : 64 * k + 32] for k in range(4)], axis=1)
        odd = jnp.concatenate([rows[:, 64 * k + 32 : 64 * k + 64] for k in range(4)], axis=1)
        keep_ref[p] = jnp.where(core == 0, even, odd)
        give_ref[p] = jnp.where(core == 0, odd, even)


def pack_body(g_ref, panel_ref, low_ref, high_ref):
    odd = place()[2] == 1
    for p in range(4):
        panel_ref[p] = jnp.concatenate([g_ref[p, :256], g_ref[p, 256:]], axis=1)
    low_ref[...] = jnp.where(odd, panel_ref[3], panel_ref[0])
    high_ref[...] = jnp.where(odd, panel_ref[0], panel_ref[3])


def write_plane(own, other, out_ref, lane):
    halves = [chip_panel(place()[1], own[:, i : i + 64], other[:, i : i + 64]) for i in (0, 64)]
    block = jnp.concatenate(halves, axis=0)
    edge = jnp.zeros((16, 1, 128), F32)
    blank = jnp.zeros((32, 128), BF16)
    cells = block.astype(F32).reshape(16, 32, 128)
    moved = (
        jnp.concatenate([cells[:, 1:], edge], axis=1).reshape(512, 128).astype(BF16),
        block,
        jnp.concatenate([edge, cells[:, :31]], axis=1).reshape(512, 128).astype(BF16),
    )
    for c in range(3):
        out_ref[c, 0:32, lane : lane + 128] = blank
        out_ref[c, 32:544, lane : lane + 128] = moved[c]
        out_ref[c, 544:576, lane : lane + 128] = blank


def inner_body(panel_ref, other_ref, x_ref, out_ref, keep_ref, give_ref, token_ref):
    for p in range(4):
        keep_ref[p] = split_channels(place()[1], x_ref[p], True)
        give_ref[p] = split_channels(place()[1], x_ref[p], False)
    for p in range(4):
        write_plane(panel_ref[p], other_ref[p], out_ref, 128 * p)
    token_ref[...] = jnp.zeros((8, 128), F32)


def write_edges(inner_ref, rims, edge_ref):
    edge_ref[0, :, :, 128:] = inner_ref[:, :, :128]
    edge_ref[1, :, :, :128] = inner_ref[:, :, 384:]
    write_plane(rims[0][0], rims[1][0], edge_ref.at[0], 0)
    write_plane(rims[0][1], rims[1][1], edge_ref.at[1], 128)


def window(bc):
    return slice(64 - 32 * (bc // 3), 576 - 32 * (bc // 3))


def patches(inner_ref, edge_ref, t, i, bc):
    return inner_ref[bc % 3, window(bc), 128:384] if t != i else edge_ref[t, bc % 3, window(bc), :]


def split_channels(core, block, own):
    parts = [
        jnp.concatenate([block[:, 64 * k + 32 * h : 64 * k + 32 * h + 32] for k in range(4)], axis=1) for h in range(2)
    ]
    return jnp.where((core == 0) == own, parts[0], parts[1])


def pair_body(first_ref, second_ref, out_ref):
    odd = place()[2] == 1
    out_ref[0] = jnp.where(odd, second_ref[...], first_ref[...])
    out_ref[1] = jnp.where(odd, first_ref[...], second_ref[...])


def give_body(_, *refs):
    for i in range(3):
        for p in range(4):
            refs[3][i, p] = split_channels(place()[1], refs[i][p], False)


def kernel_grad_body(inner_ref, *refs):
    rims, keep_ref, blocks, own_got_ref, got_ref, out_ref, token_ref, rim_ref, x_ref, xt_ref, sum_ref = (
        refs[:2], refs[2], refs[3:6], *refs[6:]
    )
    for i in range(2):
        write_plane(rims[0][i], rims[1][i], rim_ref.at[i], 0)
    chip, core, _ = place()
    for i in range(8):
        spot = 2 * lax.rem(chip + (0, 3, 1, 2)[i % 4], 4) + (core if i < 4 else 1 - core)
        for p in range(4):
            if i % 4 == 0:
                part = (own_got_ref if i else keep_ref)[p]
            else:
                part = split_channels(place()[1], blocks[i - 1][p], True) if i < 4 else got_ref[i - 5, p]
            rows = pl.ds(pl.multiple_of(512 * (p // 2) + spot * 64, 64), 64)
            x_ref[rows, 128 * (p % 2) : 128 * (p % 2) + 128] = part
    token_ref[...] = jnp.zeros((8, 128), F32)
    for i in range(2):
        xt_ref[128 * i : 128 * (i + 1), :] = x_ref[:, 128 * i : 128 * (i + 1)].T
    most = jnp.zeros((128, 128), F32)
    low, high = xt_ref.at[:, :512], xt_ref.at[:, 512:]
    ends = (low.at[:128], high.at[:128], low.at[128:], high.at[128:])

    def multiply(left_ref, right):
        return jnp.dot(left_ref[...], right, preferred_element_type=F32)

    for start in range(0, 9, 2):
        taps = range(start, min(start + 2, 9))

        def beside(read):
            return jnp.concatenate([read(bc % 3, window(bc)) for bc in taps], axis=1)

        up = multiply(ends[1], beside(lambda c, cells: inner_ref[c, cells, 128:256]))
        up = up + multiply(ends[0], beside(lambda c, cells: rim_ref[0, c, cells, :]))
        down = multiply(ends[2], beside(lambda c, cells: inner_ref[c, cells, 256:384]))
        down = down + multiply(ends[3], beside(lambda c, cells: rim_ref[1, c, cells, :]))
        for i, bc in enumerate(taps):
            one = slice(128 * i, 128 * i + 128)
            first = multiply(low, inner_ref[bc % 3, window(bc), 0:256])
            last = multiply(high, inner_ref[bc % 3, window(bc), 256:512])
            totals = (
                (first[:128, 128:] + last[:128, 128:]) + down[:, one],
                (first[:128, :128] + first[128:, 128:]) + (last[:128, :128] + last[128:, 128:]),
                (first[128:, :128] + last[128:, :128]) + up[:, one],
            )
            for a in range(3):
                total = totals[a] * (32768.0**-0.5)
                sum_ref[9 * a + bc] = total
                most = jnp.maximum(most, jnp.abs(total))
    exponent = top_exponent(most)
    for k in range(27):
        sum_ref[k] = encode(sum_ref[k], exponent)
    stamp = jnp.broadcast_to(exponent, (2, 128))
    for jr in range(4):
        for k in range(4):
            rows = slice(32 * k + 8 * jr, 32 * k + 8 * jr + 8)
            rest = jnp.concatenate([sum_ref[24 + i, rows, :] for i in range(3)], axis=0)
            for jt in range(4):
                tiles = [sum_ref[6 * jt + i, rows, :] for i in range(6)] + [rest[6 * jt : 6 * jt + 6], stamp]
                out_ref[(4 * jr + jt) * 4 + k] = jnp.concatenate(tiles, axis=0).astype(BF16)


def shard_sum_body(in_ref, _, out_ref, sum_ref):
    used = lax.broadcasted_iota(jnp.int32, (56, 128), 0) < 54
    most = jnp.zeros((56, 128), F32)
    for k in range(4):
        total = jnp.zeros((56, 128), F32)
        for j in range(16):
            code = in_ref[4 * j + k].astype(F32)
            total = total + decode(code, code[54:55])
        total = jnp.where(used, total, 0.0)
        sum_ref[k] = total
        most = jnp.maximum(most, jnp.abs(total))
    exponent = top_exponent(most)
    for k in range(4):
        code = jnp.where(used, encode(sum_ref[k], exponent), exponent).astype(BF16)
        for j in range(16):
            out_ref[j, k] = code


def kernel_out_body(in_ref, out_ref):
    for jr in range(4):
        for k in range(4):
            at = (slice(8 * jr, 8 * jr + 8), slice(128 * k, 128 * (k + 1)))
            rest = []
            for jt in range(4):
                code = in_ref[4 * jr + jt, k].astype(F32)
                value = decode(code, code[54:55])
                for i in range(6):
                    out_ref[6 * jt + i, at[0], at[1]] = value[8 * i : 8 * i + 8]
                rest.append(value[48:54])
            rest = jnp.concatenate(rest, axis=0)
            for i in range(3):
                out_ref[24 + i, at[0], at[1]] = rest[8 * i : 8 * i + 8]


def data_grad_body(inner_ref, rims_ref, rims_other_ref, weight_ref, _, *refs):
    outs, token_ref, cut_ref, w_ref, edge_ref, sem = refs[:4], *refs[4:9]
    chip, core, _ = place()
    copy = pltpu.make_async_copy(weight_ref.at[:, :, pl.ds(pl.multiple_of(chip * 128, 128), 128)], cut_ref, sem)
    copy.start()
    write_edges(inner_ref, (rims_ref, rims_other_ref), edge_ref)
    token_ref[...] = jnp.zeros((8, 128), F32)
    copy.wait()
    none = jnp.zeros((32, 128), BF16)
    for d in range(4):
        rows = pl.ds(pl.multiple_of(64 * lax.rem(chip + d, 4) + 32 * core, 32), 32)
        for bc in range(9):
            for e in range(2):
                for slot in range(4):
                    a = e + 2 - slot
                    lanes = slice(512 * bc + 128 * slot, 512 * bc + 128 * slot + 128)
                    w_ref[128 * e + 32 * d : 128 * e + 32 * d + 32, lanes] = (
                        cut_ref[9 * a + bc, rows, :] if 0 <= a < 3 else none
                    )
    planes = []
    for t in range(2):
        prod = jnp.zeros((512, 256), F32)
        for bc in range(9):
            for i in range(2):
                prod = prod + lax.dot_general(
                    patches(inner_ref, edge_ref, t, i, bc), w_ref[:, 512 * bc + 256 * i : 512 * bc + 256 * i + 256],
                    (((1,), (1,)), ((), ())), preferred_element_type=F32,
                )
        planes += [prod[:, :128], prod[:, 128:]]
    for d, out_ref in enumerate(outs):
        slab = jnp.concatenate([plane[:, 32 * d : 32 * (d + 1)] for plane in planes], axis=1)
        if d == 0:
            out_ref[...] = slab
        else:
            exponent = top_exponent(jnp.abs(slab))
            out_ref[:512, :] = encode(slab, exponent).astype(BF16)
            out_ref[512:, :] = jnp.broadcast_to(exponent, (16, 128)).astype(BF16)


def data_out_body(own_ref, *refs):
    total = own_ref[...]
    for ref in refs[:3]:
        code = ref[...].astype(F32)
        total = total + decode(code[:512], code[512:513])
    for p in range(4):
        refs[3][p] = total[:, 32 * p : 32 * (p + 1)]


def on_device(activations, out_grad, weight):
    struct = jax.ShapeDtypeStruct
    whole = ("samp", "vox", "chan")
    cores = [[8 * j + 2 * k + h for j in range(16) for k in range(4)] for h in range(2)]

    def hop(value, chips, cores):
        return lax.ppermute(
            value, "chan", [(i, ((i // 2 + chips) % 4) * 2 + (i % 2 ^ cores)) for i in range(8)]
        )

    x = activations.reshape(4, 64, 256)
    g = out_grad.reshape(4, 512, 64)
    near = [hop(x, d, 0) for d in (1, 3, 2)]
    rim, token = struct((256, 128), BF16), struct((8, 128), F32)
    panel, low, high = call(pack_body, (struct((4, 256, 128), BF16), rim, rim), [VM])(g)
    left = lax.ppermute(low, "vox", [swap for i in (1, 3, 5) for swap in ((i, i + 1), (i + 1, i))])
    right = lax.ppermute(high, "vox", [swap for i in (0, 2, 4, 6) for swap in ((i, i + 1), (i + 1, i))])
    other = hop(panel, 0, 1)
    rims = call(pair_body, struct((2, 256, 128), BF16), [VM, VM], nbytes=PAIR)(left, right)
    rims = [rims, hop(rims, 0, 1)]
    kept = struct((4, 64, 128), BF16)
    inner, keep, own_give, built = call(
        inner_body, (struct((3, 576, 512), BF16), kept, kept, token), [VM, VM, VM], nbytes=TINY
    )(panel, other, x)
    own_got = hop(own_give, 0, 1)
    give = call(give_body, struct((3, 4, 64, 128), BF16), [VM] * 4, nbytes=TINY)(built, *near)
    got = hop(give, 0, 1)

    edges = pltpu.VMEM((2, 3, 576, 256), BF16)
    codes, made = call(
        kernel_grad_body, (struct((64, 56, 128), BF16), token), [VM] * 9,
        [pltpu.VMEM((2, 3, 576, 128), BF16), pltpu.VMEM((1024, 256), BF16), pltpu.VMEM((256, 1024), BF16), pltpu.VMEM((27, 128, 128), F32)],
        2 * 2304 * 1024 * 512, 12 << 20, 12,
    )(inner, *rims, keep, *near, own_got, got)
    swapped = lax.all_to_all(codes, whole, split_axis=0, concat_axis=0, tiled=True, axis_index_groups=cores)
    slab, coded = struct((512, 128), F32), struct((528, 128), BF16)
    *slabs, done = call(
        data_grad_body, (slab, coded, coded, coded, token), [VM] * 3 + [HBM, VM],
        [pltpu.VMEM((27, 256, 128), BF16), pltpu.VMEM((256, 4608), BF16), edges, pltpu.SemaphoreType.DMA],
        2 * 2304 * 1024 * 512, 12 << 20, 24,
    )(inner, *rims, weight, made)
    shards = call(
        shard_sum_body, struct((16, 4, 56, 128), BF16), [VM, VM], [pltpu.VMEM((4, 56, 128), F32)]
    )(swapped, done)
    final = lax.all_to_all(shards, ("samp", "vox"), split_axis=0, concat_axis=0, tiled=True)
    weight_grad = call(kernel_out_body, struct((27, 32, 512), F32), [VM])(final)
    data_grad = call(data_out_body, struct((4, 512, 32), F32), [VM] * 4)(
        slabs[0], *[hop(slabs[d], d, 0) for d in (1, 3, 2)]
    )
    return data_grad.reshape(1, 4, 16, 32, 32), weight_grad


def solution(mesh):
    placed = (P("samp", "vox", "chan", None, None), P("samp", "vox", None, None, "chan"), P())
    return jax.shard_map(
        on_device,
        mesh=mesh,
        in_specs=placed,
        out_specs=(P("samp", "vox", None, None, "chan"), P(None, "chan", None)),
        check_vma=False,
    )
```

```python
import jax
import jax.numpy as jnp
from jax import lax
from jax.experimental import pallas as pl
from jax.experimental.pallas import tpu as pltpu
from jax.sharding import PartitionSpec as P

F32, BF16 = jnp.float32, jnp.bfloat16
STEPS, BIAS = 249.0, 125.0
TINY = 1024
PAIR = 11070000
VM = pl.BlockSpec(memory_space=pltpu.VMEM)
HBM = pl.BlockSpec(memory_space=pltpu.HBM)


def place():
    chan = lax.axis_index("chan")
    return lax.div(chan, 2), lax.rem(chan, 2), lax.rem(lax.axis_index("vox"), 2)


def call(body, outs, ins, scratch=(), flops=0, nbytes=1 << 20, mib=4, specs=None):
    return pl.pallas_call(
        body,
        out_shape=outs,
        in_specs=ins,
        out_specs=specs or jax.tree.map(lambda _: VM, outs),
        scratch_shapes=list(scratch),
        compiler_params=pltpu.CompilerParams(vmem_limit_bytes=mib << 20),
        cost_estimate=pl.CostEstimate(flops=flops, bytes_accessed=nbytes, transcendentals=0),
    )


def encode(value, exponent):
    size = jnp.abs(value) * jnp.exp2(-exponent) + 1e-30
    code = jnp.exp2(size * lax.rsqrt(size) * STEPS - BIAS)
    return jnp.where(value < 0, -code, code)


def decode(code, exponent):
    q = jnp.log2(jnp.abs(code)) + BIAS
    square = q * q * (jnp.exp2(exponent) / (STEPS * STEPS))
    return jnp.where(code < 0, -square, square)


def top_exponent(most):
    most = jnp.max(jnp.max(most, axis=0, keepdims=True), axis=1, keepdims=True)
    return jnp.ceil(jnp.log2(jnp.maximum(most, 1e-30)))


def chip_panel(core, own, other):
    return jnp.where(core == 0, jnp.concatenate([own, other], axis=1), jnp.concatenate([other, own], axis=1))


def split_channels(core, block, keep_ref, give_ref):
    for p in range(4):
        rows = block[p]
        even = jnp.concatenate([rows[:, 64 * k : 64 * k + 32] for k in range(4)], axis=1)
        odd = jnp.concatenate([rows[:, 64 * k + 32 : 64 * k + 64] for k in range(4)], axis=1)
        keep_ref[p] = jnp.where(core == 0, even, odd)
        give_ref[p] = jnp.where(core == 0, odd, even)


def pack_body(g_ref, panel_ref, low_ref, high_ref):
    odd = place()[2] == 1
    for p in range(4):
        panel_ref[p] = jnp.concatenate([g_ref[p, :256], g_ref[p, 256:]], axis=1)
    low_ref[...] = jnp.where(odd, panel_ref[3], panel_ref[0])
    high_ref[...] = jnp.where(odd, panel_ref[0], panel_ref[3])


def write_plane(own, other, out_ref, lane):
    halves = [chip_panel(place()[1], own[:, i : i + 64], other[:, i : i + 64]) for i in (0, 64)]
    block = jnp.concatenate(halves, axis=0)
    edge = jnp.zeros((16, 1, 128), F32)
    blank = jnp.zeros((32, 128), BF16)
    cells = block.astype(F32).reshape(16, 32, 128)
    moved = (
        jnp.concatenate([cells[:, 1:], edge], axis=1).reshape(512, 128).astype(BF16),
        block,
        jnp.concatenate([edge, cells[:, :31]], axis=1).reshape(512, 128).astype(BF16),
    )
    for c in range(3):
        out_ref[c, 0:32, lane : lane + 128] = blank
        out_ref[c, 32:544, lane : lane + 128] = moved[c]
        out_ref[c, 544:576, lane : lane + 128] = blank


def inner_body(panel_ref, other_ref, x_ref, out_ref, keep_ref, give_ref, token_ref):
    for p in range(4):
        keep_ref[p] = split_channels(place()[1], x_ref[p], True)
        give_ref[p] = split_channels(place()[1], x_ref[p], False)
    for p in range(4):
        write_plane(panel_ref[p], other_ref[p], out_ref, 128 * p)
    token_ref[...] = jnp.zeros((8, 128), F32)


def write_edges(inner_ref, rims, edge_ref):
    edge_ref[0, :, :, 128:] = inner_ref[:, :, :128]
    edge_ref[1, :, :, :128] = inner_ref[:, :, 384:]
    write_plane(rims[0][0], rims[1][0], edge_ref.at[0], 0)
    write_plane(rims[0][1], rims[1][1], edge_ref.at[1], 128)


def window(bc):
    return slice(64 - 32 * (bc // 3), 576 - 32 * (bc // 3))


def patches(inner_ref, edge_ref, t, i, bc):
    return inner_ref[bc % 3, window(bc), 128:384] if t != i else edge_ref[t, bc % 3, window(bc), :]


def split_channels(core, block, own):
    parts = [
        jnp.concatenate([block[:, 64 * k + 32 * h : 64 * k + 32 * h + 32] for k in range(4)], axis=1) for h in range(2)
    ]
    return jnp.where((core == 0) == own, parts[0], parts[1])


def pair_body(first_ref, second_ref, out_ref):
    odd = place()[2] == 1
    out_ref[0] = jnp.where(odd, second_ref[...], first_ref[...])
    out_ref[1] = jnp.where(odd, first_ref[...], second_ref[...])


def give_body(_, *refs):
    for i in range(3):
        for p in range(4):
            refs[3][i, p] = split_channels(place()[1], refs[i][p], False)


def kernel_grad_body(inner_ref, *refs):
    rims, keep_ref, blocks, own_got_ref, got_ref, out_ref, token_ref, rim_ref, x_ref, xt_ref, sum_ref = (
        refs[:2], refs[2], refs[3:6], *refs[6:]
    )
    for i in range(2):
        write_plane(rims[0][i], rims[1][i], rim_ref.at[i], 0)
    chip, core, _ = place()
    for i in range(8):
        spot = 2 * lax.rem(chip + (0, 3, 1, 2)[i % 4], 4) + (core if i < 4 else 1 - core)
        for p in range(4):
            if i % 4 == 0:
                part = (own_got_ref if i else keep_ref)[p]
            else:
                part = split_channels(place()[1], blocks[i - 1][p], True) if i < 4 else got_ref[i - 5, p]
            rows = pl.ds(pl.multiple_of(512 * (p // 2) + spot * 64, 64), 64)
            x_ref[rows, 128 * (p % 2) : 128 * (p % 2) + 128] = part
    token_ref[...] = jnp.zeros((8, 128), F32)
    for i in range(2):
        xt_ref[128 * i : 128 * (i + 1), :] = x_ref[:, 128 * i : 128 * (i + 1)].T
    most = jnp.zeros((128, 128), F32)
    low, high = xt_ref.at[:, :512], xt_ref.at[:, 512:]
    ends = (low.at[:128], high.at[:128], low.at[128:], high.at[128:])

    def multiply(left_ref, right):
        return jnp.dot(left_ref[...], right, preferred_element_type=F32)

    for start in range(0, 9, 2):
        taps = range(start, min(start + 2, 9))

        def beside(read):
            return jnp.concatenate([read(bc % 3, window(bc)) for bc in taps], axis=1)

        up = multiply(ends[1], beside(lambda c, cells: inner_ref[c, cells, 128:256]))
        up = up + multiply(ends[0], beside(lambda c, cells: rim_ref[0, c, cells, :]))
        down = multiply(ends[2], beside(lambda c, cells: inner_ref[c, cells, 256:384]))
        down = down + multiply(ends[3], beside(lambda c, cells: rim_ref[1, c, cells, :]))
        for i, bc in enumerate(taps):
            one = slice(128 * i, 128 * i + 128)
            first = multiply(low, inner_ref[bc % 3, window(bc), 0:256])
            last = multiply(high, inner_ref[bc % 3, window(bc), 256:512])
            totals = (
                (first[:128, 128:] + last[:128, 128:]) + down[:, one],
                (first[:128, :128] + first[128:, 128:]) + (last[:128, :128] + last[128:, 128:]),
                (first[128:, :128] + last[128:, :128]) + up[:, one],
            )
            for a in range(3):
                total = totals[a] * (32768.0**-0.5)
                sum_ref[9 * a + bc] = total
                most = jnp.maximum(most, jnp.abs(total))
    exponent = top_exponent(most)
    for k in range(27):
        sum_ref[k] = encode(sum_ref[k], exponent)
    stamp = jnp.broadcast_to(exponent, (2, 128))
    for jr in range(4):
        for k in range(4):
            rows = slice(32 * k + 8 * jr, 32 * k + 8 * jr + 8)
            rest = jnp.concatenate([sum_ref[24 + i, rows, :] for i in range(3)], axis=0)
            for jt in range(4):
                tiles = [sum_ref[6 * jt + i, rows, :] for i in range(6)] + [rest[6 * jt : 6 * jt + 6], stamp]
                out_ref[(4 * jr + jt) * 4 + k] = jnp.concatenate(tiles, axis=0).astype(BF16)


def shard_sum_body(in_ref, _, out_ref, sum_ref):
    used = lax.broadcasted_iota(jnp.int32, (56, 128), 0) < 54
    most = jnp.zeros((56, 128), F32)
    for k in range(4):
        total = jnp.zeros((56, 128), F32)
        for j in range(16):
            code = in_ref[4 * j + k].astype(F32)
            total = total + decode(code, code[54:55])
        total = jnp.where(used, total, 0.0)
        sum_ref[k] = total
        most = jnp.maximum(most, jnp.abs(total))
    exponent = top_exponent(most)
    for k in range(4):
        code = jnp.where(used, encode(sum_ref[k], exponent), exponent).astype(BF16)
        for j in range(16):
            out_ref[j, k] = code


def kernel_out_body(in_ref, out_ref, hold_ref, sems):
    copies = []
    for jr in range(4):
        rows = slice(8 * jr, 8 * jr + 8)
        for k in range(4):
            lanes = slice(128 * k, 128 * (k + 1))
            rest = []
            for jt in range(4):
                code = in_ref[4 * jr + jt, k].astype(F32)
                value = decode(code, code[54:55])
                for i in range(6):
                    hold_ref[6 * jt + i, rows, lanes] = value[8 * i : 8 * i + 8]
                rest.append(value[48:54])
            rest = jnp.concatenate(rest, axis=0)
            for i in range(3):
                hold_ref[24 + i, rows, lanes] = rest[8 * i : 8 * i + 8]
        part = pl.ds(8 * jr, 8)
        copies.append(pltpu.make_async_copy(hold_ref.at[:, part, :], out_ref.at[:, part, :], sems.at[jr]))
        copies[-1].start()
    for copy in copies:
        copy.wait()


def data_grad_body(inner_ref, rims_ref, rims_other_ref, weight_ref, _, *refs):
    outs, token_ref, cut_ref, w_ref, edge_ref, sem = refs[:4], *refs[4:9]
    chip, core, _ = place()
    copy = pltpu.make_async_copy(weight_ref.at[:, :, pl.ds(pl.multiple_of(chip * 128, 128), 128)], cut_ref, sem)
    copy.start()
    write_edges(inner_ref, (rims_ref, rims_other_ref), edge_ref)
    token_ref[...] = jnp.zeros((8, 128), F32)
    copy.wait()
    none = jnp.zeros((32, 128), BF16)
    for d in range(4):
        rows = pl.ds(pl.multiple_of(64 * lax.rem(chip + d, 4) + 32 * core, 32), 32)
        for bc in range(9):
            for e in range(2):
                for slot in range(4):
                    a = e + 2 - slot
                    lanes = slice(512 * bc + 128 * slot, 512 * bc + 128 * slot + 128)
                    w_ref[128 * e + 32 * d : 128 * e + 32 * d + 32, lanes] = (
                        cut_ref[9 * a + bc, rows, :] if 0 <= a < 3 else none
                    )
    planes = []
    for t in range(2):
        prod = jnp.zeros((512, 256), F32)
        for bc in range(9):
            for i in range(2):
                prod = prod + lax.dot_general(
                    patches(inner_ref, edge_ref, t, i, bc), w_ref[:, 512 * bc + 256 * i : 512 * bc + 256 * i + 256],
                    (((1,), (1,)), ((), ())), preferred_element_type=F32,
                )
        planes += [prod[:, :128], prod[:, 128:]]
    for d, out_ref in enumerate(outs):
        slab = jnp.concatenate([plane[:, 32 * d : 32 * (d + 1)] for plane in planes], axis=1)
        if d == 0:
            out_ref[...] = slab
        else:
            exponent = top_exponent(jnp.abs(slab))
            out_ref[:512, :] = encode(slab, exponent).astype(BF16)
            out_ref[512:, :] = jnp.broadcast_to(exponent, (16, 128)).astype(BF16)


def data_out_body(own_ref, *refs):
    total = own_ref[...]
    for ref in refs[:3]:
        code = ref[...].astype(F32)
        total = total + decode(code[:512], code[512:513])
    for p in range(4):
        refs[3][p] = total[:, 32 * p : 32 * (p + 1)]


def on_device(activations, out_grad, weight):
    struct = jax.ShapeDtypeStruct
    whole = ("samp", "vox", "chan")
    cores = [[8 * j + 2 * k + h for j in range(16) for k in range(4)] for h in range(2)]

    def hop(value, chips, cores):
        return lax.ppermute(
            value, "chan", [(i, ((i // 2 + chips) % 4) * 2 + (i % 2 ^ cores)) for i in range(8)]
        )

    x = activations.reshape(4, 64, 256)
    g = out_grad.reshape(4, 512, 64)
    near = [hop(x, d, 0) for d in (1, 3, 2)]
    rim, token = struct((256, 128), BF16), struct((8, 128), F32)
    panel, low, high = call(pack_body, (struct((4, 256, 128), BF16), rim, rim), [VM])(g)
    left = lax.ppermute(low, "vox", [swap for i in (1, 3, 5) for swap in ((i, i + 1), (i + 1, i))])
    right = lax.ppermute(high, "vox", [swap for i in (0, 2, 4, 6) for swap in ((i, i + 1), (i + 1, i))])
    other = hop(panel, 0, 1)
    rims = call(pair_body, struct((2, 256, 128), BF16), [VM, VM], nbytes=PAIR)(left, right)
    rims = [rims, hop(rims, 0, 1)]
    kept = struct((4, 64, 128), BF16)
    inner, keep, own_give, built = call(
        inner_body, (struct((3, 576, 512), BF16), kept, kept, token), [VM, VM, VM], nbytes=TINY
    )(panel, other, x)
    own_got = hop(own_give, 0, 1)
    give = call(give_body, struct((3, 4, 64, 128), BF16), [VM] * 4, nbytes=TINY)(built, *near)
    got = hop(give, 0, 1)

    edges = pltpu.VMEM((2, 3, 576, 256), BF16)
    codes, made = call(
        kernel_grad_body, (struct((64, 56, 128), BF16), token), [VM] * 9,
        [pltpu.VMEM((2, 3, 576, 128), BF16), pltpu.VMEM((1024, 256), BF16), pltpu.VMEM((256, 1024), BF16), pltpu.VMEM((27, 128, 128), F32)],
        2 * 2304 * 1024 * 512, 12 << 20, 12,
    )(inner, *rims, keep, *near, own_got, got)
    swapped = lax.all_to_all(codes, whole, split_axis=0, concat_axis=0, tiled=True, axis_index_groups=cores)
    slab, coded = struct((512, 128), F32), struct((528, 128), BF16)
    *slabs, done = call(
        data_grad_body, (slab, coded, coded, coded, token), [VM] * 3 + [HBM, VM],
        [pltpu.VMEM((27, 256, 128), BF16), pltpu.VMEM((256, 4608), BF16), edges, pltpu.SemaphoreType.DMA],
        2 * 2304 * 1024 * 512, 12 << 20, 24,
    )(inner, *rims, weight, made)
    shards = call(
        shard_sum_body, struct((16, 4, 56, 128), BF16), [VM, VM], [pltpu.VMEM((4, 56, 128), F32)]
    )(swapped, done)
    final = lax.all_to_all(shards, ("samp", "vox"), split_axis=0, concat_axis=0, tiled=True)
    weight_grad = call(
        kernel_out_body, struct((27, 32, 512), F32), [VM],
        [pltpu.VMEM((27, 32, 512), F32), pltpu.SemaphoreType.DMA((4,))], mib=6, specs=HBM,
    )(final)
    data_grad = call(data_out_body, struct((4, 512, 32), F32), [VM] * 4)(
        slabs[0], *[hop(slabs[d], d, 0) for d in (1, 3, 2)]
    )
    return data_grad.reshape(1, 4, 16, 32, 32), weight_grad


def solution(mesh):
    placed = (P("samp", "vox", "chan", None, None), P("samp", "vox", None, None, "chan"), P())
    return jax.shard_map(
        on_device,
        mesh=mesh,
        in_specs=placed,
        out_specs=(P("samp", "vox", None, None, "chan"), P(None, "chan", None)),
        check_vma=False,
    )
```
